128 devices in a mesh: tm: 4 (over x_hi, core), space: 32 (over z, y, x_lo).
Axes of the slice: x: 4 (x_hi: 2, x_lo: 2; x = x_hi * 2 + x_lo), y: 4, z: 4, core: 2. Of those that a mesh axis runs over, the one named last changes fastest.
Arguments:
- vorticity: float32 [128, 2048, 2048], P('tm', 'space'), may hold values from -6 to 6
Outputs:
- spectrum: float32 [128, 256, 256], P(None, ('tm', 'space'))
The draws below stay inside these ranges and needn't reach their ends.
All inputs are finite; a program needn't handle non-finite values.
Results may differ from the reference program's by a relative error of at most 0.000071.
Values sent between devices are 32-bit elements; how exact they have to be, the bound alone decides.
A program may use at most 128 MiB of HBM per device.

```python
import jax
import jax.numpy as jnp
from jax import lax

N = 2048
T_SIZE = 128
K = 256


def shard_levels(own_key, shape, cuts, smallest, largest):
    level = 1.0
    for axis_at, parts in cuts:
        heights = jax.random.uniform(jax.random.fold_in(jax.random.fold_in(own_key, 6), axis_at), (parts,), jnp.float32, smallest / len(cuts), largest / len(cuts))
        level = level * jnp.repeat(jnp.exp(heights), shape[axis_at] // parts).reshape((-1,) + (1,) * (len(shape) - 1 - axis_at))
    return level


def normal_values(stream_key, extent, width, most, shards=(), held_as=jnp.bfloat16):
    values = jax.random.normal(stream_key, extent, jnp.float32) * width
    if len(shards) > 0:
        values = shard_levels(stream_key, extent, shards, -0.22, 0.18) * values
    return jnp.clip(values, min=-most, max=most).astype(held_as)


def setup_inputs(seed: int = 0) -> dict:
    seeds = jax.random.split(jax.random.key(seed), 2)
    vorticity = normal_values(seeds[0], (T_SIZE, N, N), 1.0, 6.0, ((0, 4), (1, 32)), jnp.float32)
    return dict(vorticity=vorticity)


def one_snapshot(field):
    along_y = jnp.fft.fft(field, axis=1)[:, :K]
    both = jnp.fft.fft(along_y, axis=0)
    rows = (jnp.arange(K, dtype=jnp.int32) - K // 2) % N
    return both[rows] / N


def reference(vorticity):
    fourier = lax.map(one_snapshot, vorticity)
    steps = jnp.arange(T_SIZE, dtype=jnp.float32)
    taper = 0.5 - 0.5 * jnp.cos(2.0 * jnp.pi * steps / T_SIZE)
    series = jnp.fft.fft(fourier * taper[:, None, None], axis=0)
    power = jnp.real(series) ** 2 + jnp.imag(series) ** 2
    return (power / jnp.sum(taper * taper)).astype(jnp.float32)
```

```python
import functools

import jax
import jax.numpy as jnp
import ml_dtypes
import numpy as np
from jax import lax
from jax.experimental import pallas as pl
from jax.experimental.pallas import tpu as pltpu
from jax.sharding import PartitionSpec as P

N = 2048
T_SIZE = 128
K = 256
MESH = pl.DeviceIdType.MESH
F32, BF16 = jnp.float32, jnp.bfloat16
STEPS = 8


def halves(a):
    hi = a.astype(np.float32).astype(ml_dtypes.bfloat16)
    lo = (a - hi.astype(np.float64)).astype(np.float32).astype(ml_dtypes.bfloat16)
    return np.stack([hi, lo])


def turn(product, period):
    angle = (product % period) * (2.0 * np.pi / period)
    return np.cos(angle), np.sin(angle)


@functools.cache
def tables():
    cell = np.arange(N // 2)[:, None]
    rows = []
    for parity in range(2):
        c, s = turn(cell * (2 * np.arange(K // 2) + parity)[None, :], N)
        rows.append(halves(np.concatenate([c, -s], axis=1)))
    rows = np.stack(rows)
    columns = []
    for half in range(2):
        b, x, tm, a, i = np.meshgrid(
            np.arange(4), np.arange(2), np.arange(4), np.arange(4), np.arange(2), indexing="ij"
        )
        z, y = (a, b) if half == 0 else (b, a)
        wave = (64 * tm + 16 * z + 4 * y + 2 * x + i - K // 2).reshape(-1, 1)
        sets = []
        for own_b in range(4):
            for own_x in range(2):
                src, r = np.meshgrid(np.arange(4), np.arange(64), indexing="ij")
                z, y = (src, own_b) if half == 0 else (own_b, src)
                grid = (64 * (8 * z + 2 * y + own_x) + r).reshape(1, -1)
                c, s = turn(wave * grid, N)
                sets.append(halves(np.concatenate([c, s], axis=0)))
        columns.append(np.stack(sets))
    t = np.arange(T_SIZE)
    taper = 0.5 - 0.5 * np.cos(2.0 * np.pi * t / T_SIZE)
    scale = taper / N / np.sqrt(np.sum(taper * taper))
    tm, a, j = np.meshgrid(np.arange(4), np.arange(4), np.arange(8), indexing="ij")
    when = (32 * tm + 4 * j + a).reshape(-1)
    c, s = turn(np.arange(T_SIZE)[:, None] * when[None, :], T_SIZE)
    eye = np.eye(2)
    time = halves(
        np.concatenate([np.kron(c * scale[when], eye), np.kron(s * scale[when], eye)], axis=0)
    )
    perm = np.zeros((K, K))
    k = np.arange(K)
    perm[(k % 2) * 128 + k // 2, k] = 1.0
    return rows, columns[0], columns[1], time, perm.astype(ml_dtypes.bfloat16)


def split(v):
    hi = v.astype(BF16)
    return hi, (v - hi.astype(F32)).astype(BF16)


def dot(a, b):
    return jnp.dot(a, b, preferred_element_type=F32)


def turned(table_hi, table_lo, data):
    hi, lo = split(data)
    both = dot(table_hi, hi) + dot(table_hi, lo) + dot(table_lo, hi)
    top, low = both[:256], both[256:]
    return top[:, :128] + low[:, 128:], top[:, 128:] - low[:, :128]


def kernel(
    v_ref, rows_ref, cola_ref, colb_ref, time_ref, perm_ref, o_ref,
    vbuf, rows, cols, time, perm,
    send1, recv1, part, hrecv, qrecv, xsend, xkeep, xrecv, fsend, frecv,
    v_sem, c_sem, s1_send, s1_recv, h_send, h_recv, q_send, q_recv, x_send, x_recv, f_send, f_recv,
):
    tm = lax.axis_index("tm")
    me = lax.axis_index("space")
    z, y, x = me // 8, (me // 2) % 4, me % 2
    first = (z, y)
    second = (y, z)

    def space(half, a, b, xx):
        return (a * 4 + b) * 2 + xx if half == 0 else (b * 4 + a) * 2 + xx

    def ring(v, d):
        return (v + d) % 4

    tables_in = [
        pltpu.make_async_copy(rows_ref, rows, c_sem.at[0]),
        pltpu.make_async_copy(cola_ref.at[y * 2 + x], cols.at[0], c_sem.at[1]),
        pltpu.make_async_copy(colb_ref.at[z * 2 + x], cols.at[1], c_sem.at[2]),
        pltpu.make_async_copy(time_ref, time, c_sem.at[3]),
        pltpu.make_async_copy(perm_ref, perm, c_sem.at[4]),
    ]

    def fetch(j):
        return pltpu.make_async_copy(v_ref.at[pl.ds(4 * j, 4)], vbuf.at[pl.ds(4 * j, 4)], v_sem.at[j])

    tables_in[0].start()
    for j in range(STEPS):
        fetch(j).start()
    for copy in tables_in[1:]:
        copy.start()

    barrier = pltpu.get_barrier_semaphore()

    def greet(tm_to, space_to):
        pl.semaphore_signal(barrier, inc=1, device_id={"tm": tm_to, "space": space_to}, device_id_type=MESH)

    greet(tm, space(0, z, y, 1 - x))

    @pl.loop(1, 16)
    def _(k):
        d = (tm * 4 + z + k) % 16
        greet(d // 4, space(0, d % 4, y, x))

    @pl.loop(0, 12)
    def _(k):
        greet((tm + k // 3) % 4, space(0, z, ring(y, 1 + k % 3), x))

    def remote(src, dst, send_sem, recv_sem, space_to, tm_to=None):
        to = {"space": space_to}
        if tm_to is not None:
            to["tm"] = tm_to
        return pltpu.make_async_remote_copy(
            src_ref=src, dst_ref=dst, send_sem=send_sem, recv_sem=recv_sem, device_id=to, device_id_type=MESH
        )

    def arrived(ref, sem):
        pltpu.make_async_copy(ref, ref, sem).wait()

    tables_in[0].wait()

    def rows_of(j):
        fetch(j).wait()
        block = vbuf[pl.ds(4 * j, 4)].reshape(256, N)
        low, high = block[:, : N // 2], block[:, N // 2 :]
        for half, folded in ((0, low + high), (1, low - high)):
            hi, lo = split(folded)
            out = dot(hi, rows[half, 0]) + dot(lo, rows[half, 0]) + dot(hi, rows[half, 1])
            send1[half, j] = out.reshape(4, 64, 256)

    def send_rows(j):
        for half in range(2):
            a, b = first[half], second[half]
            for d in (1, 3, 2):
                to = ring(a, d)
                remote(
                    send1.at[half, j, to], recv1.at[half, j, a],
                    s1_send.at[half], s1_recv.at[half, j], space(half, to, b, x),
                ).start()
            recv1[half, j, a] = send1[half, j, a]

    rows_of(0)
    pl.semaphore_wait(barrier, 28)
    send_rows(0)

    @pl.loop(1, STEPS)
    def _(j):
        rows_of(j)
        send_rows(j)

    for copy in tables_in[1:]:
        copy.wait()

    @pl.loop(0, STEPS)
    def _(j):
        for half in range(2):
            b = second[half]
            arrived(recv1.at[half, j, pl.ds(0, 3)], s1_recv.at[half, j])
            data = recv1[half, j].reshape(256, 256)
            re, im = turned(cols[half, 0], cols[half, 1], data)
            part[half, j, :, :, :128] = re.reshape(4, 64, 128)
            part[half, j, :, :, 128:] = im.reshape(4, 64, 128)
            far = ring(b, 2)
            for way in range(2):
                to = ring(b, 1 + 2 * way)
                remote(
                    part.at[half, j, far, pl.ds(32 * way, 32)], hrecv.at[half, j, way],
                    h_send.at[half], h_recv.at[half, j], space(half, first[half], to, x),
                ).start()

    @pl.loop(0, STEPS)
    def _(j):
        for half in range(2):
            b = second[half]
            arrived(hrecv.at[half, j], h_recv.at[half, j])
            for way in range(2):
                to = ring(b, 1 + 2 * way)
                at = pl.ds(32 * way, 32)
                part[half, j, to, at] = part[half, j, to, at] + hrecv[half, j, way]
                remote(
                    part.at[half, j, to], qrecv.at[half, j, way],
                    q_send.at[half], q_recv.at[half, j], space(half, first[half], to, x),
                ).start()

    @pl.loop(0, STEPS)
    def _(j):
        for half in range(2):
            b = second[half]
            arrived(qrecv.at[half, j], q_recv.at[half, j])
            for keep, at in ((xsend, pl.ds(32 * (1 - x), 32)), (xkeep, pl.ds(32 * x, 32))):
                keep[half, j] = part[half, j, b, at] + qrecv[half, j, 0, at] + qrecv[half, j, 1, at]
            remote(
                xsend.at[half, j], xrecv.at[half, j],
                x_send.at[half], x_recv.at[half, j], space(half, first[half], b, 1 - x),
            ).start()

    for half in range(2):
        for j in range(STEPS):
            arrived(xrecv.at[half, j], x_recv.at[half, j])
            whole = xkeep[half, j] + xrecv[half, j]
            for d in range(16):
                fsend[half, d, 2 * j : 2 * j + 2] = whole[2 * d : 2 * d + 2]
        a, b = first[half], second[half]
        mine = tm * 4 + a
        frecv[half, mine] = fsend[half, mine]

        @pl.loop(1, 16)
        def _(k):
            d = (mine + k) % 16
            remote(
                fsend.at[half, d], frecv.at[half, mine],
                f_send.at[half], f_recv.at[half], space(half, d % 4, b, x), d // 4,
            ).start()

    power = []
    for half in range(2):
        arrived(frecv.at[half, pl.ds(0, 15)], f_recv.at[half])
        re, im = turned(time[0], time[1], frecv[half].reshape(256, 256))
        power.append(re * re + im * im)
    both = jnp.concatenate(power, axis=1)
    hi, rest = both.astype(BF16), None
    rest = both - hi.astype(F32)
    mid = rest.astype(BF16)
    low = (rest - mid.astype(F32)).astype(BF16)
    o_ref[...] = dot(hi, perm[...]) + dot(mid, perm[...]) + dot(low, perm[...])

    for half in range(2):
        arrived(send1.at[half, :, pl.ds(0, 3)], s1_send.at[half])
        arrived(hrecv.at[half], h_send.at[half])
        arrived(qrecv.at[half], q_send.at[half])
        arrived(xsend.at[half], x_send.at[half])
        arrived(fsend.at[half, pl.ds(0, 15)], f_send.at[half])


def per_device(vorticity):
    any_spec = pl.BlockSpec(memory_space=pl.ANY)
    dma = pltpu.SemaphoreType.DMA
    out = pl.pallas_call(
        kernel,
        out_shape=jax.ShapeDtypeStruct((2 * T_SIZE, K), F32),
        in_specs=[any_spec] * 6,
        out_specs=pl.BlockSpec(memory_space=pltpu.VMEM),
        scratch_shapes=[
            pltpu.VMEM((32, 64, N), F32),
            pltpu.VMEM((2, 2, N // 2, 256), BF16),
            pltpu.VMEM((2, 2, 512, 256), BF16),
            pltpu.VMEM((2, 512, 256), BF16),
            pltpu.VMEM((K, K), BF16),
            pltpu.VMEM((2, STEPS, 4, 64, 256), F32),
            pltpu.VMEM((2, STEPS, 4, 64, 256), F32),
            pltpu.VMEM((2, STEPS, 4, 64, 256), F32),
            pltpu.VMEM((2, STEPS, 2, 32, 256), F32),
            pltpu.VMEM((2, STEPS, 2, 64, 256), F32),
            pltpu.VMEM((2, STEPS, 32, 256), F32),
            pltpu.VMEM((2, STEPS, 32, 256), F32),
            pltpu.VMEM((2, STEPS, 32, 256), F32),
            pltpu.VMEM((2, 16, 16, 256), F32),
            pltpu.VMEM((2, 16, 16, 256), F32),
            dma((STEPS,)),
            dma((5,)),
            dma((2,)), dma((2, STEPS)),
            dma((2,)), dma((2, STEPS)),
            dma((2,)), dma((2, STEPS)),
            dma((2,)), dma((2, STEPS)),
            dma((2,)), dma((2,)),
        ],
        compiler_params=pltpu.CompilerParams(
            collective_id=0, has_side_effects=True, vmem_limit_bytes=60 * 2**20
        ),
        cost_estimate=pl.CostEstimate(flops=12 * 10**9, bytes_accessed=24 * 2**20, transcendentals=0),
    )(vorticity, *(jnp.asarray(t) for t in tables()))
    return out.reshape(T_SIZE, 2, K)


def solution(mesh):
    return jax.shard_map(
        per_device,
        mesh=mesh,
        in_specs=(P("tm", "space", None),),
        out_specs=P(None, ("tm", "space"), None),
        check_vma=False,
    )
```

```python
import functools

import jax
import jax.numpy as jnp
import ml_dtypes
import numpy as np
from jax import lax
from jax.experimental import pallas as pl
from jax.experimental.pallas import tpu as pltpu
from jax.sharding import PartitionSpec as P

N = 2048
T_SIZE = 128
K = 256
MESH = pl.DeviceIdType.MESH
F32, BF16 = jnp.float32, jnp.bfloat16
STEPS = 8
EARLY, LATE = 4, 4
LAG, CROSS, GAP = 4, 4, 2


def halves(a):
    hi = a.astype(np.float32).astype(ml_dtypes.bfloat16)
    lo = (a - hi.astype(np.float64)).astype(np.float32).astype(ml_dtypes.bfloat16)
    return np.stack([hi, lo])


def turn(product, period):
    angle = (product % period) * (2.0 * np.pi / period)
    return np.cos(angle), np.sin(angle)


@functools.cache
def tables():
    cell = np.arange(N // 2)[:, None]
    rows = []
    for parity in range(2):
        c, s = turn(cell * (2 * np.arange(K // 2) + parity)[None, :], N)
        rows.append(halves(np.concatenate([c, -s], axis=1)))
    rows = np.stack(rows)
    columns = []
    for half in range(2):
        b, x, tm, a, i = np.meshgrid(
            np.arange(4), np.arange(2), np.arange(4), np.arange(4), np.arange(2), indexing="ij"
        )
        z, y = (a, b) if half == 0 else (b, a)
        wave = (64 * tm + 16 * z + 4 * y + 2 * x + i - K // 2).reshape(-1, 1)
        sets = []
        for own_b in range(4):
            for own_x in range(2):
                src, r = np.meshgrid(np.arange(4), np.arange(64), indexing="ij")
                z, y = (src, own_b) if half == 0 else (own_b, src)
                grid = (64 * (8 * z + 2 * y + own_x) + r).reshape(1, -1)
                c, s = turn(wave * grid, N)
                sets.append(halves(np.concatenate([c, s], axis=0)))
        columns.append(np.stack(sets))
    t = np.arange(T_SIZE)
    taper = 0.5 - 0.5 * np.cos(2.0 * np.pi * t / T_SIZE)
    scale = taper / N / np.sqrt(np.sum(taper * taper))
    group, tm, a, j = np.meshgrid(np.arange(2), np.arange(4), np.arange(4), np.arange(4), indexing="ij")
    when = (32 * tm + 4 * (4 * group + j) + a).reshape(-1)
    c, s = turn(np.arange(T_SIZE)[:, None] * when[None, :], T_SIZE)
    eye = np.eye(2)
    time = halves(
        np.concatenate([np.kron(c * scale[when], eye), np.kron(s * scale[when], eye)], axis=0)
    )
    perm = np.zeros((K, K))
    k = np.arange(K)
    perm[(k % 2) * 128 + k // 2, k] = 1.0
    return rows, columns[0], columns[1], time, perm.astype(ml_dtypes.bfloat16)


def split(v):
    hi = v.astype(BF16)
    return hi, (v - hi.astype(F32)).astype(BF16)


def dot(a, b):
    return jnp.dot(a, b, preferred_element_type=F32)


def turned(table_hi, table_lo, data):
    hi, lo = split(data)
    both = dot(table_hi, hi) + dot(table_hi, lo) + dot(table_lo, hi)
    top, low = both[:256], both[256:]
    return top[:, :128] + low[:, 128:], top[:, 128:] - low[:, :128]


def kernel(
    v_ref, rows_ref, cola_ref, colb_ref, time_ref, perm_ref, o_ref,
    vbuf, rows, cols, time, perm,
    send1, recv1, part, wrecv, erecv, grecv, hrecv, qrecv, xsend, xkeep, xrecv, fsend, frecv,
    v_sem, c_sem, s1_send, s1_recv, w_send, w_recv, e_send, e_recv, g_send, g_recv,
    h_send, h_recv, q_send, q_recv, x_send, x_recv, f_send, f_recv, relay,
):
    tm = lax.axis_index("tm")
    me = lax.axis_index("space")
    z, y, x = me // 8, (me // 2) % 4, me % 2
    own, other = pl.ds(32 * x, 32), pl.ds(32 * (1 - x), 32)
    first = (z, y)
    second = (y, z)

    def space(half, a, b, xx):
        return (a * 4 + b) * 2 + xx if half == 0 else (b * 4 + a) * 2 + xx

    def ring(v, d):
        return (v + d) % 4

    tables_in = [
        pltpu.make_async_copy(rows_ref, rows, c_sem.at[0]),
        pltpu.make_async_copy(cola_ref.at[y * 2 + x], cols.at[0], c_sem.at[1]),
        pltpu.make_async_copy(colb_ref.at[z * 2 + x], cols.at[1], c_sem.at[2]),
        pltpu.make_async_copy(time_ref, time, c_sem.at[3]),
        pltpu.make_async_copy(perm_ref, perm, c_sem.at[4]),
    ]

    def fetch(j):
        return pltpu.make_async_copy(v_ref.at[pl.ds(4 * j, 4)], vbuf.at[pl.ds(4 * j, 4)], v_sem.at[j])

    tables_in[0].start()
    fetch(0).start()

    barrier = pltpu.get_barrier_semaphore()

    def signal(sem, tm_to, space_to):
        pl.semaphore_signal(sem, inc=1, device_id={"tm": tm_to, "space": space_to}, device_id_type=MESH)

    for d in (1, 3, 2):
        signal(barrier, tm, space(0, ring(z, d), y, x))
        signal(barrier, tm, space(0, z, ring(y, d), x))
        signal(barrier, ring(tm, d), me)
    signal(barrier, tm, space(0, z, y, 1 - x))

    def remote(src, dst, send_sem, recv_sem, space_to, tm_to=None):
        to = {"space": space_to}
        if tm_to is not None:
            to["tm"] = tm_to
        return pltpu.make_async_remote_copy(
            src_ref=src, dst_ref=dst, send_sem=send_sem, recv_sem=recv_sem, device_id=to, device_id_type=MESH
        )

    def arrived(ref, sem):
        pltpu.make_async_copy(ref, ref, sem).wait()

    tables_in[0].wait()
    fetch(0).wait()
    for j in range(1, STEPS):
        fetch(j).start()
    for copy in tables_in[1:]:
        copy.start()

    def rows_of(j):
        block = vbuf[pl.ds(4 * j, 4)].reshape(256, N)
        low, high = block[:, : N // 2], block[:, N // 2 :]
        for half, folded in ((0, low + high), (1, low - high)):
            hi, lo = split(folded)
            out = dot(hi, rows[half, 0]) + dot(lo, rows[half, 0]) + dot(hi, rows[half, 1])
            send1[half, j] = out.reshape(4, 64, 256)

    def send_rows(j):
        for half in range(2):
            a, b = first[half], second[half]
            for d in (1, 3, 2):
                to = ring(a, d)
                remote(
                    send1.at[half, j, to], recv1.at[half, j, a],
                    s1_send.at[half], s1_recv.at[half, j], space(half, to, b, x),
                ).start()
            recv1[half, j, a] = send1[half, j, a]

    rows_of(0)
    pl.semaphore_wait(barrier, 10)
    send_rows(0)
    for d in (1, 3, 2):
        signal(relay, ring(tm, d), me)

    def columns_of(j):
        for half in range(2):
            arrived(recv1.at[half, j, pl.ds(0, 3)], s1_recv.at[half, j])
            data = recv1[half, j].reshape(256, 256)
            re, im = turned(cols[half, 0], cols[half, 1], data)
            part[half, j, :, :, :128] = re.reshape(4, 64, 128)
            part[half, j, :, :, 128:] = im.reshape(4, 64, 128)

    def send_raw(j):
        for half in range(2):
            remote(
                part.at[half, j, :, other], wrecv.at[half, j],
                w_send.at[half], w_recv.at[half, j], space(half, first[half], second[half], 1 - x),
            ).start()

    def send_far(half, j, start, rows, dst, send_sem, recv_sem):
        b = second[half]
        for way in range(2):
            remote(
                part.at[half, j, ring(b, 2), pl.ds(start + rows * way, rows)], dst.at[way],
                send_sem.at[half], recv_sem, space(half, first[half], ring(b, 1 + 2 * way), x),
            ).start()

    def send_near(half, j, start, rows, got, dst, send_sem, recv_sem):
        b = second[half]
        for way in range(2):
            to = ring(b, 1 + 2 * way)
            at = pl.ds(start + rows * way, rows)
            part[half, j, to, at] = part[half, j, to, at] + got[way]
            remote(
                part.at[half, j, to, pl.ds(start, 2 * rows)], dst.at[way],
                send_sem.at[half], recv_sem, space(half, first[half], to, x),
            ).start()

    def early_far(j):
        for half in range(2):
            arrived(wrecv.at[half, j], w_recv.at[half, j])
            part[half, j, :, own] = part[half, j, :, own] + wrecv[half, j]
            send_far(half, j, 32 * x, 16, erecv.at[half, j], e_send, e_recv.at[half, j])

    def early_near(j):
        for half in range(2):
            arrived(erecv.at[half, j], e_recv.at[half, j])
            send_near(half, j, 32 * x, 16, erecv[half, j], grecv.at[half, j], g_send, g_recv.at[half, j])

    def late_near(j):
        for half in range(2):
            arrived(hrecv.at[half, j], h_recv.at[half, j])
            send_near(half, j + EARLY, 0, 32, hrecv[half, j], qrecv.at[half, j], q_send, q_recv.at[half, j])

    def late_sum(j):
        for half in range(2):
            b = second[half]
            arrived(qrecv.at[half, j], q_recv.at[half, j])
            for keep, at in ((xsend, other), (xkeep, own)):
                keep[half, j] = part[half, j + EARLY, b, at] + qrecv[half, j, 0, at] + qrecv[half, j, 1, at]
            remote(
                xsend.at[half, j], xrecv.at[half, j],
                x_send.at[half], x_recv.at[half, j], space(half, first[half], b, 1 - x),
            ).start()

    def staged(i, part_of, start, count):
        @pl.when((i >= start) & (i < start + count))
        def _():
            part_of(i - start)

    def rows_step(i):
        fetch(i + 1).wait()
        rows_of(i + 1)
        send_rows(i + 1)

    def tables_step(i):
        for copy in tables_in[1:]:
            copy.wait()

    def early_columns(j):
        columns_of(j)
        send_raw(j)

    def late_columns(j):
        columns_of(j + EARLY)
        for half in range(2):
            send_far(half, j + EARLY, 0, 32, hrecv.at[half, j], h_send, h_recv.at[half, j])

    late = LAG + EARLY

    @pl.loop(1, LAG + STEPS)
    def _(i):
        staged(i, rows_step, 1, STEPS - 1)
        staged(i, tables_step, LAG, 1)
        staged(i, early_columns, LAG, EARLY)
        staged(i, late_columns, late, LATE)
        staged(i, lambda j: early_far(0), LAG + 4, 1)
        staged(i, lambda j: early_far(1), LAG + 6, 1)

    early_far(2)
    late_near(0)
    late_near(1)
    late_near(2)
    early_near(0)
    early_near(1)
    late_near(3)
    early_near(2)
    late_sum(0)
    late_sum(1)
    early_far(3)
    late_sum(2)
    late_sum(3)
    early_near(3)

    pl.semaphore_wait(relay, 3)

    def lay_out(half, group, j, whole):
        for d in range(16):
            fsend[half, group, d, 2 * j : 2 * j + 2] = whole[2 * d : 2 * d + 2]

    def send_owned(half, group):
        a, b = first[half], second[half]
        mine = tm * 4 + a
        frecv[half, group, mine] = fsend[half, group, mine]

        @pl.loop(1, 16)
        def _(k):
            d = (mine + k) % 16
            remote(
                fsend.at[half, group, d], frecv.at[half, group, mine],
                f_send.at[half], f_recv.at[half, group], space(half, d % 4, b, x), d // 4,
            ).start()

    for group in (1, 0):
        for half in range(2):
            for j in range(4 * group, 4 * group + 4):
                if j < EARLY:
                    arrived(grecv.at[half, j], g_recv.at[half, j])
                    whole = part[half, j, second[half], own] + grecv[half, j, 0] + grecv[half, j, 1]
                else:
                    arrived(xrecv.at[half, j - EARLY], x_recv.at[half, j - EARLY])
                    whole = xkeep[half, j - EARLY] + xrecv[half, j - EARLY]
                lay_out(half, group, j % 4, whole)
            send_owned(half, group)

    power = []
    for half in range(2):
        for group in range(2):
            arrived(frecv.at[half, group, pl.ds(0, 15)], f_recv.at[half, group])
        re, im = turned(time[0], time[1], frecv[half].reshape(256, 256))
        power.append(re * re + im * im)
    both = jnp.concatenate(power, axis=1)
    hi, rest = both.astype(BF16), None
    rest = both - hi.astype(F32)
    mid = rest.astype(BF16)
    low = (rest - mid.astype(F32)).astype(BF16)
    o_ref[...] = dot(hi, perm[...]) + dot(mid, perm[...]) + dot(low, perm[...])

    for half in range(2):
        arrived(send1.at[half, :, pl.ds(0, 3)], s1_send.at[half])
        arrived(wrecv.at[half], w_send.at[half])
        arrived(erecv.at[half], e_send.at[half])
        arrived(grecv.at[half], g_send.at[half])
        arrived(hrecv.at[half], h_send.at[half])
        arrived(qrecv.at[half], q_send.at[half])
        arrived(xsend.at[half], x_send.at[half])
        arrived(fsend.at[half, :, pl.ds(0, 15)], f_send.at[half])


def per_device(vorticity):
    any_spec = pl.BlockSpec(memory_space=pl.ANY)
    dma = pltpu.SemaphoreType.DMA
    out = pl.pallas_call(
        kernel,
        out_shape=jax.ShapeDtypeStruct((2 * T_SIZE, K), F32),
        in_specs=[any_spec] * 6,
        out_specs=pl.BlockSpec(memory_space=pltpu.VMEM),
        scratch_shapes=[
            pltpu.VMEM((32, 64, N), F32),
            pltpu.VMEM((2, 2, N // 2, 256), BF16),
            pltpu.VMEM((2, 2, 512, 256), BF16),
            pltpu.VMEM((2, 512, 256), BF16),
            pltpu.VMEM((K, K), BF16),
            pltpu.VMEM((2, STEPS, 4, 64, 256), F32),
            pltpu.VMEM((2, STEPS, 4, 64, 256), F32),
            pltpu.VMEM((2, STEPS, 4, 64, 256), F32),
            pltpu.VMEM((2, EARLY, 4, 32, 256), F32),
            pltpu.VMEM((2, EARLY, 2, 16, 256), F32),
            pltpu.VMEM((2, EARLY, 2, 32, 256), F32),
            pltpu.VMEM((2, LATE, 2, 32, 256), F32),
            pltpu.VMEM((2, LATE, 2, 64, 256), F32),
            pltpu.VMEM((2, LATE, 32, 256), F32),
            pltpu.VMEM((2, LATE, 32, 256), F32),
            pltpu.VMEM((2, LATE, 32, 256), F32),
            pltpu.VMEM((2, 2, 16, 8, 256), F32),
            pltpu.VMEM((2, 2, 16, 8, 256), F32),
            dma((STEPS,)),
            dma((5,)),
            dma((2,)), dma((2, STEPS)),
            dma((2,)), dma((2, EARLY)),
            dma((2,)), dma((2, EARLY)),
            dma((2,)), dma((2, EARLY)),
            dma((2,)), dma((2, LATE)),
            dma((2,)), dma((2, LATE)),
            dma((2,)), dma((2, LATE)),
            dma((2,)), dma((2, 2)),
            pltpu.SemaphoreType.REGULAR,
        ],
        compiler_params=pltpu.CompilerParams(
            collective_id=0, has_side_effects=True, vmem_limit_bytes=60 * 2**20
        ),
        cost_estimate=pl.CostEstimate(flops=12 * 10**9, bytes_accessed=24 * 2**20, transcendentals=0),
    )(vorticity, *(jnp.asarray(t) for t in tables()))
    return out.reshape(T_SIZE, 2, K)


def solution(mesh):
    return jax.shard_map(
        per_device,
        mesh=mesh,
        in_specs=(P("tm", "space", None),),
        out_specs=P(None, ("tm", "space"), None),
        check_vma=False,
    )
```

```python
import functools

import jax
import jax.numpy as jnp
import ml_dtypes
import numpy as np
from jax import lax
from jax.experimental import pallas as pl
from jax.experimental.pallas import tpu as pltpu
from jax.sharding import PartitionSpec as P

N = 2048
T_SIZE = 128
K = 256
MESH = pl.DeviceIdType.MESH
F32, BF16 = jnp.float32, jnp.bfloat16
STEPS = 8
EARLY, LATE = 4, 4
LAG, CROSS, GAP = 4, 4, 2


def halves(a):
    hi = a.astype(np.float32).astype(ml_dtypes.bfloat16)
    lo = (a - hi.astype(np.float64)).astype(np.float32).astype(ml_dtypes.bfloat16)
    return np.stack([hi, lo])


def turn(product, period):
    angle = (product % period) * (2.0 * np.pi / period)
    return np.cos(angle), np.sin(angle)


@functools.cache
def tables():
    cell = np.arange(N // 2)[:, None]
    rows = []
    for parity in range(2):
        c, s = turn(cell * (2 * np.arange(K // 2) + parity)[None, :], N)
        rows.append(halves(np.concatenate([c, -s], axis=1)))
    rows = np.stack(rows)
    columns = []
    for half in range(2):
        b, x, tm, a, i = np.meshgrid(
            np.arange(4), np.arange(2), np.arange(4), np.arange(4), np.arange(2), indexing="ij"
        )
        z, y = (a, b) if half == 0 else (b, a)
        wave = (64 * tm + 16 * z + 4 * y + 2 * x + i - K // 2).reshape(-1, 1)
        sets = []
        for own_b in range(4):
            for own_x in range(2):
                src, r = np.meshgrid(np.arange(4), np.arange(64), indexing="ij")
                z, y = (src, own_b) if half == 0 else (own_b, src)
                grid = (64 * (8 * z + 2 * y + own_x) + r).reshape(1, -1)
                c, s = turn(wave * grid, N)
                sets.append(halves(np.concatenate([c, s], axis=0)))
        columns.append(np.stack(sets))
    t = np.arange(T_SIZE)
    taper = 0.5 - 0.5 * np.cos(2.0 * np.pi * t / T_SIZE)
    scale = taper / N / np.sqrt(np.sum(taper * taper))
    group, tm, a, j = np.meshgrid(
        np.arange(STEPS // 2), np.arange(4), np.arange(4), np.arange(2), indexing="ij"
    )
    when = (32 * tm + 4 * (2 * group + j) + a).reshape(-1)
    c, s = turn(np.arange(T_SIZE)[:, None] * when[None, :], T_SIZE)
    c, s = ((v * scale[when]).reshape(T_SIZE, -1, 1, 2) for v in (c, s))
    sides = [np.concatenate(pair, axis=2).reshape(T_SIZE, -1) for pair in ((c, s), (-s, c))]
    eye = np.eye(2)
    time = halves(np.concatenate([np.kron(side, eye) for side in sides], axis=0))
    perm = np.zeros((K, K))
    k = np.arange(K)
    perm[(k % 2) * 128 + k // 2, k] = 1.0
    return rows, columns[0], columns[1], time, perm.astype(ml_dtypes.bfloat16)


def split(v):
    hi = v.astype(BF16)
    return hi, (v - hi.astype(F32)).astype(BF16)


def dot(a, b):
    return jnp.dot(a, b, preferred_element_type=F32)


def turned(table_hi, table_lo, data):
    hi, lo = split(data)
    both = dot(table_hi, hi) + dot(table_hi, lo) + dot(table_lo, hi)
    top, low = both[:256], both[256:]
    return top[:, :128] + low[:, 128:], top[:, 128:] - low[:, :128]


def kernel(
    v_ref, rows_ref, cola_ref, colb_ref, time_ref, perm_ref, o_ref,
    vbuf, rows, cols, time, perm,
    send1, recv1, part, wrecv, erecv, grecv, hrecv, qrecv, xsend, xkeep, xrecv, fsend, frecv,
    v_sem, c_sem, s1_send, s1_recv, w_send, w_recv, e_send, e_recv, g_send, g_recv,
    h_send, h_recv, q_send, q_recv, x_send, x_recv, f_send, f_recv, relay,
):
    tm = lax.axis_index("tm")
    me = lax.axis_index("space")
    z, y, x = me // 8, (me // 2) % 4, me % 2
    own, other = pl.ds(32 * x, 32), pl.ds(32 * (1 - x), 32)
    first = (z, y)
    second = (y, z)

    def space(half, a, b, xx):
        return (a * 4 + b) * 2 + xx if half == 0 else (b * 4 + a) * 2 + xx

    def ring(v, d):
        return (v + d) % 4

    tables_in = [
        pltpu.make_async_copy(rows_ref, rows, c_sem.at[0]),
        pltpu.make_async_copy(cola_ref.at[y * 2 + x], cols.at[0], c_sem.at[1]),
        pltpu.make_async_copy(colb_ref.at[z * 2 + x], cols.at[1], c_sem.at[2]),
        pltpu.make_async_copy(time_ref, time, c_sem.at[3]),
        pltpu.make_async_copy(perm_ref, perm, c_sem.at[4]),
    ]

    def fetch(j):
        return pltpu.make_async_copy(v_ref.at[pl.ds(4 * j, 4)], vbuf.at[pl.ds(4 * j, 4)], v_sem.at[j])

    tables_in[0].start()
    fetch(0).start()

    barrier = pltpu.get_barrier_semaphore()

    def signal(sem, tm_to, space_to):
        pl.semaphore_signal(sem, inc=1, device_id={"tm": tm_to, "space": space_to}, device_id_type=MESH)

    for d in (1, 3, 2):
        signal(barrier, tm, space(0, ring(z, d), y, x))
        signal(barrier, tm, space(0, z, ring(y, d), x))
        signal(barrier, ring(tm, d), me)
    signal(barrier, tm, space(0, z, y, 1 - x))

    def remote(src, dst, send_sem, recv_sem, space_to, tm_to=None):
        to = {"space": space_to}
        if tm_to is not None:
            to["tm"] = tm_to
        return pltpu.make_async_remote_copy(
            src_ref=src, dst_ref=dst, send_sem=send_sem, recv_sem=recv_sem, device_id=to, device_id_type=MESH
        )

    def arrived(ref, sem):
        pltpu.make_async_copy(ref, ref, sem).wait()

    tables_in[0].wait()
    fetch(0).wait()
    for j in range(1, STEPS):
        fetch(j).start()
    for copy in tables_in[1:]:
        copy.start()

    def rows_of(j):
        block = vbuf[pl.ds(4 * j, 4)].reshape(256, N)
        low, high = block[:, : N // 2], block[:, N // 2 :]
        for half, folded in ((0, low + high), (1, low - high)):
            hi, lo = split(folded)
            out = dot(hi, rows[half, 0]) + dot(lo, rows[half, 0]) + dot(hi, rows[half, 1])
            send1[half, j] = out.reshape(4, 64, 256)

    def send_rows(j):
        for half in range(2):
            a, b = first[half], second[half]
            for d in (1, 3, 2):
                to = ring(a, d)
                remote(
                    send1.at[half, j, to], recv1.at[half, j, a],
                    s1_send.at[half], s1_recv.at[half, j], space(half, to, b, x),
                ).start()
            recv1[half, j, a] = send1[half, j, a]

    rows_of(0)
    pl.semaphore_wait(barrier, 10)
    send_rows(0)
    for d in (1, 3, 2):
        signal(relay, ring(tm, d), me)

    def columns_of(j):
        for half in range(2):
            arrived(recv1.at[half, j, pl.ds(0, 3)], s1_recv.at[half, j])
            data = recv1[half, j].reshape(256, 256)
            re, im = turned(cols[half, 0], cols[half, 1], data)
            part[half, j, :, :, :128] = re.reshape(4, 64, 128)
            part[half, j, :, :, 128:] = im.reshape(4, 64, 128)

    def send_raw(j):
        for half in range(2):
            remote(
                part.at[half, j, :, other], wrecv.at[half, j],
                w_send.at[half], w_recv.at[half, j], space(half, first[half], second[half], 1 - x),
            ).start()

    def send_far(half, j, start, rows, dst, send_sem, recv_sem):
        b = second[half]
        for way in range(2):
            remote(
                part.at[half, j, ring(b, 2), pl.ds(start + rows * way, rows)], dst.at[way],
                send_sem.at[half], recv_sem, space(half, first[half], ring(b, 1 + 2 * way), x),
            ).start()

    def send_near(half, j, start, rows, got, dst, send_sem, recv_sem):
        b = second[half]
        for way in range(2):
            to = ring(b, 1 + 2 * way)
            at = pl.ds(start + rows * way, rows)
            part[half, j, to, at] = part[half, j, to, at] + got[way]
            remote(
                part.at[half, j, to, pl.ds(start, 2 * rows)], dst.at[way],
                send_sem.at[half], recv_sem, space(half, first[half], to, x),
            ).start()

    def early_far(j):
        for half in range(2):
            arrived(wrecv.at[half, j], w_recv.at[half, j])
            part[half, j, :, own] = part[half, j, :, own] + wrecv[half, j]
            send_far(half, j, 32 * x, 16, erecv.at[half, j], e_send, e_recv.at[half, j])

    def early_near(j):
        for half in range(2):
            arrived(erecv.at[half, j], e_recv.at[half, j])
            send_near(half, j, 32 * x, 16, erecv[half, j], grecv.at[half, j], g_send, g_recv.at[half, j])

    def late_near(j):
        for half in range(2):
            arrived(hrecv.at[half, j], h_recv.at[half, j])
            send_near(half, j + EARLY, 0, 32, hrecv[half, j], qrecv.at[half, j], q_send, q_recv.at[half, j])

    def late_sum(j):
        for half in range(2):
            b = second[half]
            arrived(qrecv.at[half, j], q_recv.at[half, j])
            for keep, at in ((xsend, other), (xkeep, own)):
                keep[half, j] = part[half, j + EARLY, b, at] + qrecv[half, j, 0, at] + qrecv[half, j, 1, at]
            remote(
                xsend.at[half, j], xrecv.at[half, j],
                x_send.at[half], x_recv.at[half, j], space(half, first[half], b, 1 - x),
            ).start()

    def staged(i, part_of, start, count):
        @pl.when((i >= start) & (i < start + count))
        def _():
            part_of(i - start)

    def rows_step(i):
        fetch(i + 1).wait()
        rows_of(i + 1)
        send_rows(i + 1)

    def tables_step(i):
        for copy in tables_in[1:]:
            copy.wait()

    def early_columns(j):
        columns_of(j)
        send_raw(j)

    def late_columns(j):
        columns_of(j + EARLY)
        for half in range(2):
            send_far(half, j + EARLY, 0, 32, hrecv.at[half, j], h_send, h_recv.at[half, j])

    late = LAG + EARLY

    @pl.loop(1, LAG + STEPS)
    def _(i):
        staged(i, rows_step, 1, STEPS - 1)
        staged(i, tables_step, LAG, 1)
        staged(i, early_columns, LAG, EARLY)
        staged(i, late_columns, late, LATE)
        staged(i, lambda j: early_far(0), LAG + 4, 1)
        staged(i, lambda j: early_far(1), LAG + 6, 1)

    def send_owned(group):
        for half in range(2):
            for j in range(2):
                n = 2 * group + j
                if n < EARLY:
                    arrived(grecv.at[half, n], g_recv.at[half, n])
                    whole = part[half, n, second[half], own] + grecv[half, n, 0] + grecv[half, n, 1]
                else:
                    n = n - EARLY
                    arrived(xrecv.at[half, n], x_recv.at[half, n])
                    whole = xkeep[half, n] + xrecv[half, n]
                for d in range(16):
                    for side in range(2):
                        fsend[half, group, d, 4 * side + 2 * j : 4 * side + 2 * j + 2] = whole[
                            2 * d : 2 * d + 2, 128 * side : 128 * side + 128
                        ]
            a, b = first[half], second[half]
            mine = tm * 4 + a
            frecv[half, group, mine] = fsend[half, group, mine]

            @pl.loop(1, 16)
            def _(k):
                d = (mine + k) % 16
                remote(
                    fsend.at[half, group, d], frecv.at[half, group, mine],
                    f_send.at[half], f_recv.at[half, group], space(half, d % 4, b, x), d // 4,
                ).start()

    early_far(2)
    late_near(0)
    late_near(1)
    late_near(2)
    early_near(0)
    early_near(1)
    late_near(3)
    early_near(2)
    late_sum(0)
    late_sum(1)
    pl.semaphore_wait(relay, 3)
    early_far(3)
    late_sum(2)
    late_sum(3)
    early_near(3)
    send_owned(0)
    send_owned(2)
    send_owned(3)
    send_owned(1)
    for half in range(2):
        for group in range(STEPS // 2):
            arrived(frecv.at[half, group, pl.ds(0, 15)], f_recv.at[half, group])
    hi, lo = split(jnp.concatenate([frecv[half].reshape(512, 128) for half in range(2)], axis=1))
    sums = dot(time[0], hi) + dot(time[0], lo) + dot(time[1], hi)
    both = sums[:256] * sums[:256] + sums[256:] * sums[256:]
    hi = both.astype(BF16)
    rest = both - hi.astype(F32)
    mid = rest.astype(BF16)
    low = (rest - mid.astype(F32)).astype(BF16)
    o_ref[...] = dot(hi, perm[...]) + dot(mid, perm[...]) + dot(low, perm[...])

    for half in range(2):
        arrived(send1.at[half, :, pl.ds(0, 3)], s1_send.at[half])
        arrived(wrecv.at[half], w_send.at[half])
        arrived(erecv.at[half], e_send.at[half])
        arrived(grecv.at[half], g_send.at[half])
        arrived(hrecv.at[half], h_send.at[half])
        arrived(qrecv.at[half], q_send.at[half])
        arrived(xsend.at[half], x_send.at[half])
        arrived(fsend.at[half, :, pl.ds(0, 15)], f_send.at[half])


def per_device(vorticity):
    any_spec = pl.BlockSpec(memory_space=pl.ANY)
    dma = pltpu.SemaphoreType.DMA
    out = pl.pallas_call(
        kernel,
        out_shape=jax.ShapeDtypeStruct((2 * T_SIZE, K), F32),
        in_specs=[any_spec] * 6,
        out_specs=pl.BlockSpec(memory_space=pltpu.VMEM),
        scratch_shapes=[
            pltpu.VMEM((32, 64, N), F32),
            pltpu.VMEM((2, 2, N // 2, 256), BF16),
            pltpu.VMEM((2, 2, 512, 256), BF16),
            pltpu.VMEM((2, 512, 512), BF16),
            pltpu.VMEM((K, K), BF16),
            pltpu.VMEM((2, STEPS, 4, 64, 256), F32),
            pltpu.VMEM((2, STEPS, 4, 64, 256), F32),
            pltpu.VMEM((2, STEPS, 4, 64, 256), F32),
            pltpu.VMEM((2, EARLY, 4, 32, 256), F32),
            pltpu.VMEM((2, EARLY, 2, 16, 256), F32),
            pltpu.VMEM((2, EARLY, 2, 32, 256), F32),
            pltpu.VMEM((2, LATE, 2, 32, 256), F32),
            pltpu.VMEM((2, LATE, 2, 64, 256), F32),
            pltpu.VMEM((2, LATE, 32, 256), F32),
            pltpu.VMEM((2, LATE, 32, 256), F32),
            pltpu.VMEM((2, LATE, 32, 256), F32),
            pltpu.VMEM((2, STEPS // 2, 16, 8, 128), F32),
            pltpu.VMEM((2, STEPS // 2, 16, 8, 128), F32),
            dma((STEPS,)),
            dma((5,)),
            dma((2,)), dma((2, STEPS)),
            dma((2,)), dma((2, EARLY)),
            dma((2,)), dma((2, EARLY)),
            dma((2,)), dma((2, EARLY)),
            dma((2,)), dma((2, LATE)),
            dma((2,)), dma((2, LATE)),
            dma((2,)), dma((2, LATE)),
            dma((2,)), dma((2, STEPS // 2)),
            pltpu.SemaphoreType.REGULAR,
        ],
        compiler_params=pltpu.CompilerParams(
            collective_id=0, has_side_effects=True, vmem_limit_bytes=60 * 2**20
        ),
        cost_estimate=pl.CostEstimate(flops=12 * 10**9, bytes_accessed=24 * 2**20, transcendentals=0),
    )(vorticity, *(jnp.asarray(t) for t in tables()))
    return out.reshape(T_SIZE, 2, K)


def solution(mesh):
    return jax.shard_map(
        per_device,
        mesh=mesh,
        in_specs=(P("tm", "space", None),),
        out_specs=P(None, ("tm", "space"), None),
        check_vma=False,
    )
```

```python
import functools

import jax
import jax.numpy as jnp
import ml_dtypes
import numpy as np
from jax import lax
from jax.experimental import pallas as pl
from jax.experimental.pallas import tpu as pltpu
from jax.sharding import PartitionSpec as P

N = 2048
T_SIZE = 128
K = 256
MESH = pl.DeviceIdType.MESH
F32, BF16 = jnp.float32, jnp.bfloat16
STEPS = 8
ORDER = (0, 2, 3, 1)
EARLY, LATE = 4, 4
LAG, CROSS, GAP = 4, 4, 2


def halves(a):
    hi = a.astype(np.float32).astype(ml_dtypes.bfloat16)
    lo = (a - hi.astype(np.float64)).astype(np.float32).astype(ml_dtypes.bfloat16)
    return np.stack([hi, lo])


def turn(product, period):
    angle = (product % period) * (2.0 * np.pi / period)
    return np.cos(angle), np.sin(angle)


@functools.cache
def tables():
    cell = np.arange(N // 2)[:, None]
    rows = []
    for parity in range(2):
        c, s = turn(cell * (2 * np.arange(K // 2) + parity)[None, :], N)
        rows.append(halves(np.concatenate([c, -s], axis=1)))
    rows = np.stack(rows)
    columns = []
    for half in range(2):
        b, x, tm, a, i = np.meshgrid(
            np.arange(4), np.arange(2), np.arange(4), np.arange(4), np.arange(2), indexing="ij"
        )
        z, y = (a, b) if half == 0 else (b, a)
        wave = (64 * tm + 16 * z + 4 * y + 2 * x + i - K // 2).reshape(-1, 1)
        sets = []
        for own_b in range(4):
            for own_x in range(2):
                src, r = np.meshgrid(np.arange(4), np.arange(64), indexing="ij")
                z, y = (src, own_b) if half == 0 else (own_b, src)
                grid = (64 * (8 * z + 2 * y + own_x) + r).reshape(1, -1)
                c, s = turn(wave * grid, N)
                sets.append(halves(np.concatenate([c, s], axis=0)))
        columns.append(np.stack(sets))
    t = np.arange(T_SIZE)
    taper = 0.5 - 0.5 * np.cos(2.0 * np.pi * t / T_SIZE)
    scale = taper / N / np.sqrt(np.sum(taper * taper))
    group, tm, a, j = np.meshgrid(
        np.array(ORDER), np.arange(4), np.arange(4), np.arange(2), indexing="ij"
    )
    when = (32 * tm + 4 * (2 * group + j) + a).reshape(-1)
    c, s = turn(np.arange(T_SIZE)[:, None] * when[None, :], T_SIZE)
    c, s = ((v * scale[when]).reshape(T_SIZE, -1, 1, 2) for v in (c, s))
    sides = [np.concatenate(pair, axis=2).reshape(T_SIZE, -1) for pair in ((c, s), (-s, c))]
    eye = np.eye(2)
    time = halves(np.concatenate([np.kron(side, eye) for side in sides], axis=0))
    perm = np.zeros((K, K))
    k = np.arange(K)
    perm[(k % 2) * 128 + k // 2, k] = 1.0
    return rows, columns[0], columns[1], time, perm.astype(ml_dtypes.bfloat16)


def split(v):
    hi = v.astype(BF16)
    return hi, (v - hi.astype(F32)).astype(BF16)


def dot(a, b):
    return jnp.dot(a, b, preferred_element_type=F32)


def turned(table_hi, table_lo, data):
    hi, lo = split(data)
    both = dot(table_hi, hi) + dot(table_hi, lo) + dot(table_lo, hi)
    top, low = both[:256], both[256:]
    return top[:, :128] + low[:, 128:], top[:, 128:] - low[:, :128]


def kernel(
    v_ref, rows_ref, cola_ref, colb_ref, time_ref, perm_ref, o_ref,
    vbuf, rows, cols, time, perm,
    send1, recv1, part, wrecv, erecv, grecv, hrecv, qrecv, xsend, xkeep, xrecv, fsend, frecv,
    v_sem, c_sem, s1_send, s1_recv, w_send, w_recv, e_send, e_recv, g_send, g_recv,
    h_send, h_recv, q_send, q_recv, x_send, x_recv, f_send, f_recv, relay,
):
    tm = lax.axis_index("tm")
    me = lax.axis_index("space")
    z, y, x = me // 8, (me // 2) % 4, me % 2
    own, other = pl.ds(32 * x, 32), pl.ds(32 * (1 - x), 32)
    first = (z, y)
    second = (y, z)

    def space(half, a, b, xx):
        return (a * 4 + b) * 2 + xx if half == 0 else (b * 4 + a) * 2 + xx

    def ring(v, d):
        return (v + d) % 4

    tables_in = [
        pltpu.make_async_copy(rows_ref, rows, c_sem.at[0]),
        pltpu.make_async_copy(cola_ref.at[y * 2 + x], cols.at[0], c_sem.at[1]),
        pltpu.make_async_copy(colb_ref.at[z * 2 + x], cols.at[1], c_sem.at[2]),
        pltpu.make_async_copy(time_ref, time, c_sem.at[3]),
        pltpu.make_async_copy(perm_ref, perm, c_sem.at[4]),
    ]

    def fetch(j):
        return pltpu.make_async_copy(v_ref.at[pl.ds(4 * j, 4)], vbuf.at[pl.ds(4 * j, 4)], v_sem.at[j])

    barrier = pltpu.get_barrier_semaphore()

    def signal(sem, tm_to, space_to):
        pl.semaphore_signal(sem, inc=1, device_id={"tm": tm_to, "space": space_to}, device_id_type=MESH)

    for d in (1, 3, 2):
        signal(barrier, tm, space(0, ring(z, d), y, x))
        signal(barrier, tm, space(0, z, ring(y, d), x))
        signal(barrier, ring(tm, d), me)
    signal(barrier, tm, space(0, z, y, 1 - x))

    tables_in[0].start()
    fetch(0).start()

    def remote(src, dst, send_sem, recv_sem, space_to, tm_to=None):
        to = {"space": space_to}
        if tm_to is not None:
            to["tm"] = tm_to
        return pltpu.make_async_remote_copy(
            src_ref=src, dst_ref=dst, send_sem=send_sem, recv_sem=recv_sem, device_id=to, device_id_type=MESH
        )

    def arrived(ref, sem):
        pltpu.make_async_copy(ref, ref, sem).wait()

    tables_in[0].wait()
    fetch(0).wait()
    for j in range(1, STEPS):
        fetch(j).start()
    for copy in tables_in[1:]:
        copy.start()

    def rows_of(j):
        block = vbuf[pl.ds(4 * j, 4)].reshape(256, N)
        low, high = block[:, : N // 2], block[:, N // 2 :]
        for half, folded in ((0, low + high), (1, low - high)):
            hi, lo = split(folded)
            out = dot(hi, rows[half, 0]) + dot(lo, rows[half, 0]) + dot(hi, rows[half, 1])
            send1[half, j] = out.reshape(4, 64, 256)

    def send_rows(j):
        for half in range(2):
            a, b = first[half], second[half]
            for d in (1, 3, 2):
                to = ring(a, d)
                remote(
                    send1.at[half, j, to], recv1.at[half, j, a],
                    s1_send.at[half], s1_recv.at[half, j], space(half, to, b, x),
                ).start()
            recv1[half, j, a] = send1[half, j, a]

    rows_of(0)
    pl.semaphore_wait(barrier, 10)
    send_rows(0)
    for d in (1, 3, 2):
        signal(relay, ring(tm, d), me)

    def columns_of(j, then):
        for half in range(2):
            arrived(recv1.at[half, j, pl.ds(0, 3)], s1_recv.at[half, j])
            data = recv1[half, j].reshape(256, 256)
            re, im = turned(cols[half, 0], cols[half, 1], data)
            part[half, j, :, :, :128] = re.reshape(4, 64, 128)
            part[half, j, :, :, 128:] = im.reshape(4, 64, 128)
            then(half, j)

    def send_raw(half, j):
        remote(
            part.at[half, j, :, other], wrecv.at[half, j],
            w_send.at[half], w_recv.at[half, j], space(half, first[half], second[half], 1 - x),
        ).start()

    def send_far(half, j, start, rows, dst, send_sem, recv_sem):
        b = second[half]
        for way in range(2):
            remote(
                part.at[half, j, ring(b, 2), pl.ds(start + rows * way, rows)], dst.at[way],
                send_sem.at[half], recv_sem, space(half, first[half], ring(b, 1 + 2 * way), x),
            ).start()

    def send_near(half, j, start, rows, got, dst, send_sem, recv_sem):
        b = second[half]
        for way in range(2):
            to = ring(b, 1 + 2 * way)
            at = pl.ds(start + rows * way, rows)
            part[half, j, to, at] = part[half, j, to, at] + got[way]
            remote(
                part.at[half, j, to, pl.ds(start, 2 * rows)], dst.at[way],
                send_sem.at[half], recv_sem, space(half, first[half], to, x),
            ).start()

    def early_far(j):
        for half in range(2):
            arrived(wrecv.at[half, j], w_recv.at[half, j])
            part[half, j, :, own] = part[half, j, :, own] + wrecv[half, j]
            send_far(half, j, 32 * x, 16, erecv.at[half, j], e_send, e_recv.at[half, j])

    def early_near(j):
        for half in range(2):
            arrived(erecv.at[half, j], e_recv.at[half, j])
            send_near(half, j, 32 * x, 16, erecv[half, j], grecv.at[half, j], g_send, g_recv.at[half, j])

    def late_near(j):
        for half in range(2):
            arrived(hrecv.at[half, j], h_recv.at[half, j])
            send_near(half, j + EARLY, 0, 32, hrecv[half, j], qrecv.at[half, j], q_send, q_recv.at[half, j])

    def late_sum(j):
        for half in range(2):
            b = second[half]
            arrived(qrecv.at[half, j], q_recv.at[half, j])
            for keep, at in ((xsend, other), (xkeep, own)):
                keep[half, j] = part[half, j + EARLY, b, at] + qrecv[half, j, 0, at] + qrecv[half, j, 1, at]
            remote(
                xsend.at[half, j], xrecv.at[half, j],
                x_send.at[half], x_recv.at[half, j], space(half, first[half], b, 1 - x),
            ).start()

    def staged(i, part_of, start, count):
        @pl.when((i >= start) & (i < start + count))
        def _():
            part_of(i - start)

    def rows_step(i):
        fetch(i + 1).wait()
        rows_of(i + 1)
        send_rows(i + 1)

    def tables_step(i):
        for copy in tables_in[1:]:
            copy.wait()

    def early_columns(j):
        columns_of(j, send_raw)

    def late_columns(j):
        columns_of(
            j + EARLY,
            lambda half, n: send_far(half, n, 0, 32, hrecv.at[half, j], h_send, h_recv.at[half, j]),
        )

    late = LAG + EARLY

    @pl.loop(1, LAG + STEPS)
    def _(i):
        staged(i, rows_step, 1, STEPS - 1)
        staged(i, tables_step, LAG, 1)
        staged(i, early_columns, LAG, EARLY)
        staged(i, late_columns, late, LATE)
        staged(i, lambda j: early_far(0), LAG + 4, 1)
        staged(i, lambda j: early_far(1), LAG + 6, 1)

    def send_owned(slot):
        group = ORDER[slot]
        for half in range(2):
            for j in range(2):
                n = 2 * group + j
                if n < EARLY:
                    arrived(grecv.at[half, n], g_recv.at[half, n])
                    whole = part[half, n, second[half], own] + grecv[half, n, 0] + grecv[half, n, 1]
                else:
                    n = n - EARLY
                    arrived(xrecv.at[half, n], x_recv.at[half, n])
                    whole = xkeep[half, n] + xrecv[half, n]
                for d in range(16):
                    for side in range(2):
                        fsend[half, slot, d, 4 * side + 2 * j : 4 * side + 2 * j + 2] = whole[
                            2 * d : 2 * d + 2, 128 * side : 128 * side + 128
                        ]
            a, b = first[half], second[half]
            mine = tm * 4 + a
            frecv[half, slot, mine] = fsend[half, slot, mine]

            @pl.loop(1, 16)
            def _(k):
                d = (mine + k) % 16
                remote(
                    fsend.at[half, slot, d], frecv.at[half, slot, mine],
                    f_send.at[half], f_recv.at[half, slot], space(half, d % 4, b, x), d // 4,
                ).start()

    early_far(2)
    late_near(0)
    late_near(1)
    late_near(2)
    early_near(0)
    early_near(1)
    late_near(3)
    early_near(2)
    late_sum(0)
    late_sum(1)
    pl.semaphore_wait(relay, 3)
    early_far(3)
    late_sum(2)
    late_sum(3)
    early_near(3)
    send_owned(0)
    send_owned(1)
    send_owned(2)
    send_owned(3)
    sums = None
    for pair in range(2):
        for half in range(2):
            for slot in (2 * pair, 2 * pair + 1):
                arrived(frecv.at[half, slot, pl.ds(0, 15)], f_recv.at[half, slot])
        data = [frecv[half, 2 * pair : 2 * pair + 2].reshape(256, 128) for half in range(2)]
        hi, lo = split(jnp.concatenate(data, axis=1))
        at = slice(256 * pair, 256 * pair + 256)
        term = dot(time[0, :, at], hi) + dot(time[0, :, at], lo) + dot(time[1, :, at], hi)
        sums = term if sums is None else sums + term
    both = sums[:256] * sums[:256] + sums[256:] * sums[256:]
    hi = both.astype(BF16)
    rest = both - hi.astype(F32)
    mid = rest.astype(BF16)
    low = (rest - mid.astype(F32)).astype(BF16)
    o_ref[...] = dot(hi, perm[...]) + dot(mid, perm[...]) + dot(low, perm[...])

    for half in range(2):
        arrived(send1.at[half, :, pl.ds(0, 3)], s1_send.at[half])
        arrived(wrecv.at[half], w_send.at[half])
        arrived(erecv.at[half], e_send.at[half])
        arrived(grecv.at[half], g_send.at[half])
        arrived(hrecv.at[half], h_send.at[half])
        arrived(qrecv.at[half], q_send.at[half])
        arrived(xsend.at[half], x_send.at[half])
        arrived(fsend.at[half, :, pl.ds(0, 15)], f_send.at[half])


def per_device(vorticity):
    any_spec = pl.BlockSpec(memory_space=pl.ANY)
    dma = pltpu.SemaphoreType.DMA
    out = pl.pallas_call(
        kernel,
        out_shape=jax.ShapeDtypeStruct((2 * T_SIZE, K), F32),
        in_specs=[any_spec] * 6,
        out_specs=pl.BlockSpec(memory_space=pltpu.VMEM),
        scratch_shapes=[
            pltpu.VMEM((32, 64, N), F32),
            pltpu.VMEM((2, 2, N // 2, 256), BF16),
            pltpu.VMEM((2, 2, 512, 256), BF16),
            pltpu.VMEM((2, 512, 512), BF16),
            pltpu.VMEM((K, K), BF16),
            pltpu.VMEM((2, STEPS, 4, 64, 256), F32),
            pltpu.VMEM((2, STEPS, 4, 64, 256), F32),
            pltpu.VMEM((2, STEPS, 4, 64, 256), F32),
            pltpu.VMEM((2, EARLY, 4, 32, 256), F32),
            pltpu.VMEM((2, EARLY, 2, 16, 256), F32),
            pltpu.VMEM((2, EARLY, 2, 32, 256), F32),
            pltpu.VMEM((2, LATE, 2, 32, 256), F32),
            pltpu.VMEM((2, LATE, 2, 64, 256), F32),
            pltpu.VMEM((2, LATE, 32, 256), F32),
            pltpu.VMEM((2, LATE, 32, 256), F32),
            pltpu.VMEM((2, LATE, 32, 256), F32),
            pltpu.VMEM((2, STEPS // 2, 16, 8, 128), F32),
            pltpu.VMEM((2, STEPS // 2, 16, 8, 128), F32),
            dma((STEPS,)),
            dma((5,)),
            dma((2,)), dma((2, STEPS)),
            dma((2,)), dma((2, EARLY)),
            dma((2,)), dma((2, EARLY)),
            dma((2,)), dma((2, EARLY)),
            dma((2,)), dma((2, LATE)),
            dma((2,)), dma((2, LATE)),
            dma((2,)), dma((2, LATE)),
            dma((2,)), dma((2, STEPS // 2)),
            pltpu.SemaphoreType.REGULAR,
        ],
        compiler_params=pltpu.CompilerParams(
            collective_id=0, has_side_effects=True, vmem_limit_bytes=60 * 2**20
        ),
        cost_estimate=pl.CostEstimate(flops=12 * 10**9, bytes_accessed=24 * 2**20, transcendentals=0),
    )(vorticity, *(jnp.asarray(t) for t in tables()))
    return out.reshape(T_SIZE, 2, K)


def solution(mesh):
    return jax.shard_map(
        per_device,
        mesh=mesh,
        in_specs=(P("tm", "space", None),),
        out_specs=P(None, ("tm", "space"), None),
        check_vma=False,
    )
```
